256 devices in a mesh: blk: 16 (over y_hi, x, core), uly: 16 (over z, y_lo).
Axes of the slice: x: 4, y: 4 (y_hi: 2, y_lo: 2; y = y_hi * 2 + y_lo), z: 8, core: 2. Of those that a mesh axis runs over, the one named last changes fastest.
Arguments:
- queries: bfloat16 [32768, 6144], P(('blk', 'uly')), may hold values from -5.5 to 5.5
- keys: bfloat16 [32768, 6144], P(('blk', 'uly')), may hold values from -5.5 to 5.5
- values: bfloat16 [32768, 6144], P(('blk', 'uly')), may hold values from -6 to 6
- key_tiles: int32 [48, 256, 12], P('uly', 'blk'), may hold values from 0 to 255, as said below
- tile_mask: int32 [48, 256, 12], P('uly', 'blk'), may hold values from 0 to 1
Outputs:
- attended: bfloat16 [32768, 6144], P(('blk', 'uly'))
The draws below stay inside these ranges and needn't reach their ends.
Inputs may be any that keep to these rules, and one draw needn't show every extreme that they name: Where tile_mask is 1, key_tiles[h, i, j] names a key tile within 8 tiles of query tile i; the tiles named with mask 1 for one query tile are distinct and always include tile i itself.
All inputs are finite; a program needn't handle non-finite values.
Results may differ from the reference program's by a relative error of at most 0.0046.
Values may be sent and summed in bfloat16 or wider, within the bound.
No kernel may reach another device: no remote copies, remote signals or barrier semaphores. Data moves between devices by JAX's collectives and lax.ppermute only.
A program may use at most 128 MiB of HBM per device.

```python
import math
import jax
import jax.numpy as jnp
from jax import lax

HEAD_DIM = 128
TILE = 128
KMAX = 12
SLAB_TILES = 16
HEADS = 48
WIDTH = 6144
TILES = 256
SEQ = 32768
REACH = 8


def draw_queries(key, part):
    key = jax.random.fold_in(key, 3)
    sample = jnp.clip(jax.random.normal(key, (SEQ, WIDTH), jnp.float32), -5.5, 5.5)
    return sample.astype(jnp.bfloat16)


def draw_keys(key, part):
    key = jax.random.fold_in(key, 5)
    sample = jnp.clip(jax.random.normal(key, (SEQ, WIDTH), jnp.float32), -5.5, 5.5)
    return sample.astype(jnp.bfloat16)


def tile_lists(key):
    pick_key, count_key, head_key, trim_key, order_key = jax.random.split(key, 5)
    others = 2 * REACH
    candidate = jnp.arange(others, dtype=jnp.int32)
    offsets = jnp.where(candidate < REACH, candidate - REACH, candidate - REACH + 1)
    ranking = jax.random.randint(pick_key, (HEADS, TILES, others), 0, 1 << 20, dtype=jnp.int32) * 1024 + candidate
    ranked_values, picked = lax.top_k(ranking, KMAX - 1)
    chosen = jnp.concatenate((jnp.zeros((HEADS, TILES, 1), jnp.int32), offsets[picked]), axis=2)
    query_tile = jnp.arange(TILES, dtype=jnp.int32)[None, :, None]
    named_tiles = query_tile + chosen
    inside = (named_tiles >= 0) & (named_tiles < TILES)
    counts = jax.random.randint(count_key, (HEADS,), (KMAX + 2) // 3, KMAX + 1, dtype=jnp.int32)
    fullest = jax.random.randint(head_key, (), 0, HEADS, dtype=jnp.int32)
    counts = jnp.where(jnp.arange(HEADS, dtype=jnp.int32) == fullest, KMAX, counts)
    trimmed = jax.random.randint(trim_key, (HEADS, TILES), 0, 3, dtype=jnp.int32)
    row_counts = jnp.clip(counts[:, None] - trimmed, 1, KMAX)
    slot_index = jnp.arange(KMAX, dtype=jnp.int32)
    usable = (slot_index[None, None, :] < row_counts[:, :, None]) & inside
    shuffle = jax.random.randint(order_key, (HEADS, TILES, KMAX), 0, 1 << 20, dtype=jnp.int32) * 1024 + slot_index
    arrangement = jnp.argsort(shuffle, axis=2)
    named_tiles = jnp.take_along_axis(named_tiles, arrangement, axis=2)
    usable = jnp.take_along_axis(usable, arrangement, axis=2)
    named_tiles = jnp.where(usable, named_tiles, query_tile)
    return (named_tiles.astype(jnp.int32), usable.astype(jnp.int32))


def draw_key_tiles(key, part):
    named_tiles, usable = tile_lists(key)
    return named_tiles


def draw_tile_mask(key, part):
    named_tiles, usable = tile_lists(key)
    return usable


def levels(own_key, shape, pieces, smallest, high):
    loudness = 1.0
    for dim, shards_of in pieces:
        steps = jax.random.uniform(jax.random.fold_in(jax.random.fold_in(own_key, 6), dim), (shards_of,), jnp.float32, smallest / len(pieces), high / len(pieces))
        loudness = loudness * jnp.repeat(jnp.exp(steps), shape[dim] // shards_of).reshape((-1,) + (1,) * (len(shape) - 1 - dim))
    return loudness


def centred(stream_key, extent, width, reach, cuts=(), kind=jnp.bfloat16):
    result = jax.random.normal(stream_key, extent, jnp.float32) * width
    if len(cuts) > 0:
        result = levels(stream_key, extent, cuts, -0.22, 0.18) * result
    return jnp.clip(result, min=-reach, max=reach).astype(kind)


def setup_inputs(seed: int = 0) -> dict:
    key_list = jax.random.split(jax.random.key(seed), 6)
    return {
        "queries": draw_queries(jax.random.fold_in(key_list[5], 71), 0),
        "keys": draw_keys(jax.random.fold_in(key_list[5], 71), 0),
        "values": centred(key_list[2], (SEQ, WIDTH), 1.0, 6.0, ((0, 256),)),
        "key_tiles": draw_key_tiles(jax.random.fold_in(key_list[5], 71), 0),
        "tile_mask": draw_tile_mask(jax.random.fold_in(key_list[5], 71), 0),
    }


def attend_group(query_block, gathered_keys, gathered_values, usable, factor):
    scores = jnp.einsum('btd,bjsd->btjs', query_block.astype(jnp.float32), gathered_keys.astype(jnp.float32)) * factor
    scores = jnp.where(usable[:, None, :, None], scores, -jnp.inf)
    highest = lax.optimization_barrier(jnp.max(scores, axis=(2, 3), keepdims=True))
    weights = jnp.exp(scores - highest)
    totals = lax.optimization_barrier(jnp.sum(weights, axis=(2, 3)))
    rounded = lax.optimization_barrier(weights.astype(jnp.bfloat16))
    summed = jnp.einsum('btjs,bjsd->btd', rounded.astype(jnp.float32), gathered_values.astype(jnp.float32))
    return (summed / totals[..., None]).astype(jnp.bfloat16)

def reference(queries, keys, values, key_tiles, tile_mask):
    factor = 1.0 / math.sqrt(HEAD_DIM)
    group_tiles = min(SLAB_TILES, 512 // TILE)

    def one_head(head_number):
        column = (head_number * HEAD_DIM).astype(jnp.int32)
        head_queries = lax.dynamic_slice_in_dim(queries, column, HEAD_DIM, 1).reshape(TILES, TILE, HEAD_DIM)
        head_keys = lax.dynamic_slice_in_dim(keys, column, HEAD_DIM, 1).reshape(TILES, TILE, HEAD_DIM)
        head_values = lax.dynamic_slice_in_dim(values, column, HEAD_DIM, 1).reshape(TILES, TILE, HEAD_DIM)
        tile_rows = key_tiles[head_number]
        usable_all = tile_mask[head_number] > 0

        def one_group(offset):
            query_block = lax.dynamic_slice_in_dim(head_queries, offset, group_tiles, 0)
            tile_block = lax.dynamic_slice_in_dim(tile_rows, offset, group_tiles, 0)
            usable = lax.dynamic_slice_in_dim(usable_all, offset, group_tiles, 0)
            return attend_group(query_block, head_keys[tile_block], head_values[tile_block], usable, factor)
        results = lax.map(one_group, jnp.arange(TILES // group_tiles, dtype=jnp.int32) * group_tiles)
        return results.reshape(SEQ, HEAD_DIM)
    per_head = lax.map(one_head, jnp.arange(HEADS, dtype=jnp.int32))
    return per_head.transpose(1, 0, 2).reshape(SEQ, HEADS * HEAD_DIM)
```

```python
import functools
import math

import jax
import jax.numpy as jnp
from jax import lax
from jax.experimental import pallas as pl
from jax.experimental.pallas import tpu as pltpu
from jax.sharding import PartitionSpec as P

TILE = 128
HEAD_DIM = 128
REACH = 8
HEAD_SETS = (2, 1)
VMEM_LIMIT = 48 * 1024 * 1024


def passed_along(x, axis, by):
    length = lax.axis_size(axis)
    pairs = [(i, i + by) for i in range(length) if 0 <= i + by < length]
    return lax.ppermute(x, axis, pairs)


def exchanged(x):
    return lax.all_to_all(x, "uly", split_axis=0, concat_axis=0, tiled=True)


def pack_kernel(widths, *refs):
    inputs, outputs = refs[:3], refs[3:]
    for which, ref in enumerate(inputs):
        per_group = sum(widths)
        for group in range(ref.shape[1] // per_group):
            column = group * per_group
            for out, width in zip(outputs, widths):
                out[group, which] = ref[:, column : column + width]
                column += width


def pack(queries, keys, values, groups, widths):
    per_step = 4
    columns = per_step * sum(widths)
    return pl.pallas_call(
        functools.partial(pack_kernel, widths),
        grid=(groups // per_step,),
        in_specs=[pl.BlockSpec((TILE, columns), lambda g: (0, g))] * 3,
        out_specs=[
            pl.BlockSpec((per_step, 3, TILE, width), lambda g: (g, 0, 0, 0)) for width in widths
        ],
        out_shape=[
            jax.ShapeDtypeStruct((groups, 3, TILE, width), jnp.bfloat16) for width in widths
        ],
        compiler_params=pltpu.CompilerParams(vmem_limit_bytes=VMEM_LIMIT),
        name="pack",
    )(queries, keys, values)


def unpack_kernel(widths, *refs):
    inputs, out = refs[:-1], refs[-1]
    per_group = sum(widths)
    for group in range(out.shape[1] // per_group):
        column = group * per_group
        for ref, width in zip(inputs, widths):
            out[:, column : column + width] = ref[group]
            column += width


def unpack(parts, groups, widths):
    per_step = 4
    columns = per_step * sum(widths)
    return pl.pallas_call(
        functools.partial(unpack_kernel, widths),
        grid=(groups // per_step,),
        in_specs=[
            pl.BlockSpec((per_step, TILE, width), lambda g: (g, 0, 0)) for width in widths
        ],
        out_specs=pl.BlockSpec((TILE, columns), lambda g: (0, g)),
        out_shape=jax.ShapeDtypeStruct((TILE, groups * sum(widths)), jnp.bfloat16),
        compiler_params=pltpu.CompilerParams(vmem_limit_bytes=VMEM_LIMIT),
        name="unpack",
    )(*parts)


def attend_kernel(
    heads, slots, tile_ref, mask_ref, own, earlier, further, out, query, window, sems
):
    slab_tiles = own.shape[0]
    reach = earlier.shape[0]
    copies = [
        pltpu.make_async_copy(own.at[:, 0], query, sems.at[0]),
        pltpu.make_async_copy(
            own.at[:, pl.ds(1, 2)], window.at[pl.ds(reach, slab_tiles)], sems.at[1]
        ),
        pltpu.make_async_copy(earlier, window.at[pl.ds(0, reach)], sems.at[2]),
        pltpu.make_async_copy(further, window.at[pl.ds(reach + slab_tiles, reach)], sems.at[3]),
    ]
    for copy in copies:
        copy.start()
    for copy in copies:
        copy.wait()
    factor = math.log2(math.e) / math.sqrt(HEAD_DIM)

    def one_tile(i, carry):
        for head in range(heads):
            lanes = pl.ds(head * HEAD_DIM, HEAD_DIM)
            first = (head * slab_tiles + i) * slots
            indices = [tile_ref[first + j] for j in range(slots)]
            shut = [
                jnp.where(mask_ref[first + j] > 0, 0.0, -jnp.inf).astype(jnp.float32)
                for j in range(slots)
            ]
            tile_queries = query[i, :, lanes]
            scores = []
            for j in range(slots):
                product = lax.dot_general(
                    tile_queries,
                    window[indices[j], 0, :, lanes],
                    (((1,), (1,)), ((), ())),
                    preferred_element_type=jnp.float32,
                )
                scores.append(product * factor + shut[j])
            highest = jnp.max(functools.reduce(jnp.maximum, scores), axis=1, keepdims=True)
            weights = [jnp.exp2(score - highest) for score in scores]
            totals = jnp.sum(functools.reduce(jnp.add, weights), axis=1, keepdims=True)
            summed = jnp.dot(
                jnp.concatenate([weight.astype(jnp.bfloat16) for weight in weights], axis=1),
                jnp.concatenate([window[index, 1, :, lanes] for index in indices], axis=0),
                preferred_element_type=jnp.float32,
            )
            out[i, :, lanes] = (summed / totals).astype(jnp.bfloat16)
        return carry

    lax.fori_loop(0, slab_tiles, one_tile, 0)


def attend(tiles, mask, own, earlier, further):
    heads, slab_tiles, slots = tiles.shape
    width = own.shape[-1]
    reach = earlier.shape[0]
    window_tiles = slab_tiles + 2 * reach
    pairs = heads * slab_tiles * slots
    return pl.pallas_call(
        functools.partial(attend_kernel, heads, slots),
        in_specs=[pl.BlockSpec(memory_space=pltpu.SMEM)] * 2
        + [pl.BlockSpec(memory_space=pl.ANY)] * 3,
        out_specs=pl.BlockSpec(memory_space=pltpu.VMEM),
        out_shape=jax.ShapeDtypeStruct((slab_tiles, TILE, width), jnp.bfloat16),
        scratch_shapes=[
            pltpu.VMEM((slab_tiles, TILE, width), jnp.bfloat16),
            pltpu.VMEM((window_tiles, 2, TILE, width), jnp.bfloat16),
            pltpu.SemaphoreType.DMA((4,)),
        ],
        compiler_params=pltpu.CompilerParams(vmem_limit_bytes=VMEM_LIMIT),
        cost_estimate=pl.CostEstimate(
            flops=4 * pairs * TILE * TILE * HEAD_DIM,
            bytes_accessed=2 * TILE * width * (2 * slab_tiles + 2 * window_tiles),
            transcendentals=pairs * TILE * TILE,
        ),
        name="attend",
    )(tiles.reshape(-1), mask.reshape(-1), own, earlier, further)


def on_device(queries, keys, values, key_tiles, tile_mask):
    slab_tiles = key_tiles.shape[1]
    groups = lax.axis_size("uly")
    first_tile = lax.axis_index("blk") * slab_tiles - REACH
    local_tiles = jnp.clip(key_tiles - first_tile, 0, slab_tiles + 2 * REACH - 1)
    widths = [heads * HEAD_DIM for heads in HEAD_SETS]
    packed = pack(queries, keys, values, groups, widths)
    received = []
    for part in packed:
        if received:
            part, received[-1] = lax.optimization_barrier((part, received[-1]))
        received.append(exchanged(part))
    results = []
    head = 0
    for heads, own in zip(HEAD_SETS, received):
        earlier = passed_along(own[slab_tiles - REACH :, 1:], "blk", 1)
        further = passed_along(own[:REACH, 1:], "blk", -1)
        attended = attend(
            local_tiles[head : head + heads],
            tile_mask[head : head + heads],
            own,
            earlier,
            further,
        )
        head += heads
        results.append(exchanged(attended))
    return unpack(results, groups, widths)


def solution(mesh):
    placed = (
        P(("blk", "uly"), None),
        P(("blk", "uly"), None),
        P(("blk", "uly"), None),
        P("uly", "blk", None),
        P("uly", "blk", None),
    )
    return jax.shard_map(
        on_device, mesh=mesh, in_specs=placed, out_specs=P(("blk", "uly"), None), check_vma=False
    )
```

```python
import functools
import math

import jax
import jax.numpy as jnp
from jax import lax
from jax.experimental import pallas as pl
from jax.experimental.pallas import tpu as pltpu
from jax.sharding import PartitionSpec as P

TILE = 128
HEAD_DIM = 128
HEAD_SETS = (2, 1)
REACH = 8
PACK_VMEM = 12 * 1024 * 1024
FIRST_PACK_VMEM = 63 * 1024 * 1024
ATTEND_VMEM = 24 * 1024 * 1024


def flipped(slab, slabs):
    return slab // (slabs // 2)


def to_neighbour(x, by):
    slabs, groups = lax.axis_size("blk"), lax.axis_size("uly")
    pairs = []
    for slab in range(slabs):
        other = slab + by
        if 0 <= other < slabs:
            turn = flipped(slab, slabs) ^ flipped(other, slabs)
            for device in range(groups):
                pairs.append((slab * groups + device, other * groups + (device ^ turn)))
    return lax.ppermute(x, ("blk", "uly"), pairs)


def to_holder(x):
    slabs, groups = lax.axis_size("blk"), lax.axis_size("uly")
    pairs = [
        (slab * groups + device, slab * groups + (device ^ flipped(slab, slabs)))
        for slab in range(slabs)
        for device in range(groups)
    ]
    return lax.ppermute(x, ("blk", "uly"), pairs)


def exchanged(x):
    return lax.all_to_all(x, "uly", split_axis=0, concat_axis=0, tiled=True)


def pack_kernel(per_group, skipped, chunks, turn_ref, *refs):
    inputs, (out, held, arrived, left) = refs[:3], refs[3:]
    groups, width = out.shape[0], out.shape[-1]
    per_chunk = groups // chunks
    span = per_chunk * per_group
    taken, sent = [], []
    for chunk in range(chunks):
        for which, ref in enumerate(inputs):
            here = pl.ds(chunk * span, span)
            copy = pltpu.make_async_copy(
                ref.at[:, here], held.at[which, :, here], arrived.at[which, chunk]
            )
            copy.start()
            taken.append((chunk, which, copy))
    for chunk, which, copy in taken:
        copy.wait()
        for group in range(chunk * per_chunk, (chunk + 1) * per_chunk):
            copy = pltpu.make_async_copy(
                held.at[which, :, pl.ds(group * per_group + skipped, width)],
                out.at[group ^ turn_ref[0], which],
                left.at[which, group],
            )
            copy.start()
            sent.append(copy)
    for copy in sent:
        copy.wait()


def pack(inputs, turn, groups, skipped, width, vmem):
    chunks = 4
    rows, columns = inputs[0].shape
    return pl.pallas_call(
        functools.partial(pack_kernel, columns // groups, skipped, chunks),
        in_specs=[pl.BlockSpec(memory_space=pltpu.SMEM)]
        + [pl.BlockSpec(memory_space=pltpu.HBM)] * 3,
        out_specs=pl.BlockSpec(memory_space=pltpu.HBM),
        out_shape=jax.ShapeDtypeStruct((groups, 3, rows, width), jnp.bfloat16),
        scratch_shapes=[
            pltpu.VMEM((3, rows, columns), jnp.bfloat16),
            pltpu.SemaphoreType.DMA((3, chunks)),
            pltpu.SemaphoreType.DMA((3, groups)),
        ],
        compiler_params=pltpu.CompilerParams(vmem_limit_bytes=vmem),
        cost_estimate=pl.CostEstimate(
            flops=0, bytes_accessed=2 * 3 * rows * (columns + groups * width), transcendentals=0
        ),
        name="pack",
    )(turn, *inputs)


def unpack_kernel(widths, turn_ref, *refs):
    inputs, out = refs[:-1], refs[-1]
    per_group = sum(widths)
    for group in range(out.shape[1] // per_group):
        column = group * per_group
        for ref, width in zip(inputs, widths):
            out[:, column : column + width] = ref[group ^ turn_ref[0]]
            column += width


def unpack(parts, turn, groups):
    widths = [part.shape[-1] for part in parts]
    per_step = 4
    columns = per_step * sum(widths)
    return pl.pallas_call(
        functools.partial(unpack_kernel, widths),
        grid=(groups // per_step,),
        in_specs=[pl.BlockSpec(memory_space=pltpu.SMEM)]
        + [pl.BlockSpec((per_step, TILE, width), lambda g: (g, 0, 0)) for width in widths],
        out_specs=pl.BlockSpec((TILE, columns), lambda g: (0, g)),
        out_shape=jax.ShapeDtypeStruct((TILE, groups * sum(widths)), jnp.bfloat16),
        compiler_params=pltpu.CompilerParams(vmem_limit_bytes=PACK_VMEM),
        name="unpack",
    )(turn, *parts)


def attend_kernel(
    slots, list_ref, own, earlier, further, out, query, key, value, counted, result, scores, highest, sems
):
    slab_tiles, _, _, width = own.shape
    window_tiles = slab_tiles + 2 * REACH
    copies = [pltpu.make_async_copy(own.at[:, 0], query, sems.at[0])]
    for source, first, where in (
        (earlier, 0, pl.ds(0, REACH)),
        (own, 1, pl.ds(REACH, slab_tiles)),
        (further, 0, pl.ds(REACH + slab_tiles, REACH)),
    ):
        for which, window in enumerate((key, value)):
            copies.append(
                pltpu.make_async_copy(
                    source.at[:, first + which], window.at[where], sems.at[len(copies)]
                )
            )
    for copy in copies:
        copy.start()
    value[window_tiles] = jnp.zeros((TILE, width), jnp.bfloat16)
    counted[0] = jnp.zeros((TILE, HEAD_DIM), jnp.bfloat16)
    counted[1] = jnp.ones((TILE, HEAD_DIM), jnp.bfloat16)
    for copy in copies:
        copy.wait()
    factor = math.log2(math.e) / math.sqrt(HEAD_DIM)

    def listed(i, head):
        return [list_ref[(head * slab_tiles + i) * slots + j] for j in range(slots)]

    def score(slot, i, head):
        here = pl.ds(head * HEAD_DIM, HEAD_DIM)
        key_from = [jnp.where(n >= 0, n, i + REACH) for n in listed(i, head)]
        tile_queries = query[i, :, here]
        products = []
        for j in range(0, slots, 2):
            both = jnp.concatenate([key[key_from[j], :, here], key[key_from[j + 1], :, here]], axis=0)
            product = lax.dot_general(
                tile_queries, both, (((1,), (1,)), ((), ())), preferred_element_type=jnp.float32
            )
            scores[slot, j // 2] = product
            products.append(product)
        top = jnp.max(functools.reduce(jnp.maximum, products), axis=1, keepdims=True)
        highest[slot] = jnp.broadcast_to(top * factor, (TILE, HEAD_DIM))

    def finish(slot, i, head):
        here = pl.ds(head * HEAD_DIM, HEAD_DIM)
        named = listed(i, head)
        value_from = [jnp.where(n >= 0, n, window_tiles) for n in named]
        ones_from = [jnp.where(n >= 0, 1, 0) for n in named]
        top = jnp.concatenate([highest[slot]] * 2, axis=1)
        weights = [
            jnp.exp2(scores[slot, j] * factor - top).astype(jnp.bfloat16)
            for j in range(slots // 2)
        ]
        summed = jnp.dot(
            jnp.concatenate(weights, axis=1),
            jnp.concatenate(
                [
                    jnp.concatenate([value[v, :, here], counted[o]], axis=1)
                    for v, o in zip(value_from, ones_from)
                ],
                axis=0,
            ),
            preferred_element_type=jnp.float32,
        )
        result[i, :, here] = (summed[:, :HEAD_DIM] / summed[:, HEAD_DIM:]).astype(jnp.bfloat16)

    heads = width // HEAD_DIM
    together = 16 // heads
    steps = [(tile, head) for tile in range(together) for head in range(heads)]
    score(0, 0, 0)

    def some_tiles(n, carry):
        first = n * together
        for number, (tile, head) in enumerate(steps):
            ahead_tile, ahead_head = (steps + [(together, 0)])[number + 1]
            score((number + 1) % 2, jnp.minimum(first + ahead_tile, slab_tiles - 1), ahead_head)
            finish(number % 2, first + tile, head)
        return carry

    lax.fori_loop(0, slab_tiles // together, some_tiles, 0)
    copy = pltpu.make_async_copy(result, out, sems.at[len(copies)])
    copy.start()
    copy.wait()


def attend(lists, own, earlier, further):
    heads, slab_tiles, slots = lists.shape
    window_tiles = slab_tiles + 2 * REACH
    width = heads * HEAD_DIM
    pairs = heads * slab_tiles * slots
    return pl.pallas_call(
        functools.partial(attend_kernel, slots),
        in_specs=[pl.BlockSpec(memory_space=pltpu.SMEM)]
        + [pl.BlockSpec(memory_space=pl.ANY)] * 3,
        out_specs=pl.BlockSpec(memory_space=pl.ANY),
        out_shape=jax.ShapeDtypeStruct((slab_tiles, TILE, width), jnp.bfloat16),
        scratch_shapes=[
            pltpu.VMEM((slab_tiles, TILE, width), jnp.bfloat16),
            pltpu.VMEM((window_tiles, TILE, width), jnp.bfloat16),
            pltpu.VMEM((window_tiles + 1, TILE, width), jnp.bfloat16),
            pltpu.VMEM((2, TILE, HEAD_DIM), jnp.bfloat16),
            pltpu.VMEM((slab_tiles, TILE, width), jnp.bfloat16),
            pltpu.VMEM((2, slots // 2, TILE, 2 * TILE), jnp.float32),
            pltpu.VMEM((2, TILE, HEAD_DIM), jnp.float32),
            pltpu.SemaphoreType.DMA((8,)),
        ],
        compiler_params=pltpu.CompilerParams(vmem_limit_bytes=ATTEND_VMEM),
        cost_estimate=pl.CostEstimate(
            flops=4 * pairs * TILE * TILE * HEAD_DIM,
            bytes_accessed=2 * TILE * width * (2 * slab_tiles + 2 * window_tiles),
            transcendentals=pairs * TILE * TILE,
        ),
        name="attend",
    )(lists.reshape(-1), own, earlier, further)


def on_device(queries, keys, values, key_tiles, tile_mask):
    slab_tiles = key_tiles.shape[1]
    groups = lax.axis_size("uly")
    slab = lax.axis_index("blk")
    turn = flipped(slab, lax.axis_size("blk")).astype(jnp.int32).reshape(1)
    first_tile = slab * slab_tiles - REACH
    lists = jnp.clip(key_tiles - first_tile, 0, slab_tiles + 2 * REACH - 1)
    lists = to_holder(jnp.where(tile_mask > 0, lists, -1))
    received = []
    skipped = 0
    for heads in HEAD_SETS:
        width = heads * HEAD_DIM
        vmem = PACK_VMEM if received else FIRST_PACK_VMEM
        packed = pack((queries, keys, values), turn, groups, skipped, width, vmem)
        skipped += width
        if received:
            packed, received[-1] = lax.optimization_barrier((packed, received[-1]))
        received.append(exchanged(packed))
    results = []
    head = 0
    for heads, own in zip(HEAD_SETS, received):
        earlier = to_neighbour(own[slab_tiles - REACH :, 1:], 1)
        further = to_neighbour(own[:REACH, 1:], -1)
        results.append(exchanged(attend(lists[head : head + heads], own, earlier, further)))
        head += heads
    return unpack(results, turn, groups)


def solution(mesh):
    placed = (
        P(("blk", "uly"), None),
        P(("blk", "uly"), None),
        P(("blk", "uly"), None),
        P("uly", "blk", None),
        P("uly", "blk", None),
    )
    return jax.shard_map(
        on_device, mesh=mesh, in_specs=placed, out_specs=P(("blk", "uly"), None), check_vma=False
    )
```

```python
import functools
import math

import jax
import jax.numpy as jnp
from jax import lax
from jax.experimental import pallas as pl
from jax.experimental.pallas import tpu as pltpu
from jax.sharding import PartitionSpec as P

TILE = 128
HEAD_DIM = 128
HEAD_SETS = (2, 1)
REACH = 8
PACK_VMEM = 12 * 1024 * 1024
FIRST_PACK_VMEM = 63 * 1024 * 1024
ATTEND_VMEM = 24 * 1024 * 1024


def flipped(slab, slabs):
    return slab // (slabs // 2)


def to_neighbour(x, by):
    slabs, groups = lax.axis_size("blk"), lax.axis_size("uly")
    pairs = []
    for slab in range(slabs):
        other = slab + by
        if 0 <= other < slabs:
            turn = flipped(slab, slabs) ^ flipped(other, slabs)
            for device in range(groups):
                pairs.append((slab * groups + device, other * groups + (device ^ turn)))
    return lax.ppermute(x, ("blk", "uly"), pairs)


def to_holder(x):
    slabs, groups = lax.axis_size("blk"), lax.axis_size("uly")
    pairs = [
        (slab * groups + device, slab * groups + (device ^ flipped(slab, slabs)))
        for slab in range(slabs)
        for device in range(groups)
    ]
    return lax.ppermute(x, ("blk", "uly"), pairs)


def exchanged(x):
    return lax.all_to_all(x, "uly", split_axis=0, concat_axis=0, tiled=True)


def pack_kernel(per_group, skipped, turn_ref, *refs):
    inputs, (out, held, arrived, left) = refs[:3], refs[3:]
    groups, width = out.shape[0], out.shape[-1]
    taken = [
        pltpu.make_async_copy(ref, held.at[which], arrived.at[which])
        for which, ref in enumerate(inputs)
    ]
    for copy in taken:
        copy.start()
    sent = []
    for which, copy in enumerate(taken):
        copy.wait()
        for group in range(groups):
            copy = pltpu.make_async_copy(
                held.at[which, :, pl.ds(group * per_group + skipped, width)],
                out.at[group ^ turn_ref[0], which],
                left.at[which, group],
            )
            copy.start()
            sent.append(copy)
    for copy in sent:
        copy.wait()


def pack(inputs, turn, groups, skipped, width, vmem):
    rows, columns = inputs[0].shape
    return pl.pallas_call(
        functools.partial(pack_kernel, columns // groups, skipped),
        in_specs=[pl.BlockSpec(memory_space=pltpu.SMEM)]
        + [pl.BlockSpec(memory_space=pltpu.HBM)] * 3,
        out_specs=pl.BlockSpec(memory_space=pltpu.HBM),
        out_shape=jax.ShapeDtypeStruct((groups, 3, rows, width), jnp.bfloat16),
        scratch_shapes=[
            pltpu.VMEM((3, rows, columns), jnp.bfloat16),
            pltpu.SemaphoreType.DMA((3,)),
            pltpu.SemaphoreType.DMA((3, groups)),
        ],
        compiler_params=pltpu.CompilerParams(vmem_limit_bytes=vmem),
        cost_estimate=pl.CostEstimate(
            flops=0, bytes_accessed=2 * 3 * rows * (columns + groups * width), transcendentals=0
        ),
        name="pack",
    )(turn, *inputs)


def unpack_kernel(widths, turn_ref, *refs):
    inputs, out = refs[:-1], refs[-1]
    per_group = sum(widths)
    for group in range(out.shape[1] // per_group):
        column = group * per_group
        for ref, width in zip(inputs, widths):
            out[:, column : column + width] = ref[group ^ turn_ref[0]]
            column += width


def unpack(parts, turn, groups):
    widths = [part.shape[-1] for part in parts]
    per_step = 4
    columns = per_step * sum(widths)
    return pl.pallas_call(
        functools.partial(unpack_kernel, widths),
        grid=(groups // per_step,),
        in_specs=[pl.BlockSpec(memory_space=pltpu.SMEM)]
        + [pl.BlockSpec((per_step, TILE, width), lambda g: (g, 0, 0)) for width in widths],
        out_specs=pl.BlockSpec((TILE, columns), lambda g: (0, g)),
        out_shape=jax.ShapeDtypeStruct((TILE, groups * sum(widths)), jnp.bfloat16),
        compiler_params=pltpu.CompilerParams(vmem_limit_bytes=PACK_VMEM),
        name="unpack",
    )(turn, *parts)


def attend_kernel(first_tile, tiles, slots, n_filled, list_ref, own, halo, *refs):
    out, query, key, value, counted, result, scores, highest, sems = refs[n_filled:]
    slab_tiles, _, _, width = own.shape
    window_tiles = slab_tiles + REACH
    halo_at, own_at = (0, REACH) if first_tile == 0 else (slab_tiles, 0)
    centre = first_tile + own_at
    copies = [pltpu.make_async_copy(own.at[pl.ds(first_tile, tiles), 0], query, sems.at[0])]
    for source, first, where in (
        (halo, 0, pl.ds(halo_at, REACH)),
        (own, 1, pl.ds(own_at, slab_tiles)),
    ):
        for which, window in enumerate((key, value)):
            copies.append(
                pltpu.make_async_copy(
                    source.at[:, first + which], window.at[where], sems.at[len(copies)]
                )
            )
    for copy in copies:
        copy.start()
    value[window_tiles] = jnp.zeros((TILE, width), jnp.bfloat16)
    counted[0] = jnp.zeros((TILE, HEAD_DIM), jnp.bfloat16)
    counted[1] = jnp.ones((TILE, HEAD_DIM), jnp.bfloat16)
    for copy in copies:
        copy.wait()
    factor = math.log2(math.e) / math.sqrt(HEAD_DIM)

    def listed(i, head):
        return [list_ref[(head * tiles + i) * slots + j] for j in range(slots)]

    def score(slot, i, head):
        here = pl.ds(head * HEAD_DIM, HEAD_DIM)
        key_from = [jnp.where(n >= 0, n, i + centre) for n in listed(i, head)]
        tile_queries = query[i, :, here]
        products = []
        for j in range(0, slots, 2):
            both = jnp.concatenate([key[key_from[j], :, here], key[key_from[j + 1], :, here]], axis=0)
            product = lax.dot_general(
                tile_queries, both, (((1,), (1,)), ((), ())), preferred_element_type=jnp.float32
            )
            scores[slot, j // 2] = product
            products.append(product)
        top = jnp.max(functools.reduce(jnp.maximum, products), axis=1, keepdims=True)
        highest[slot] = jnp.broadcast_to(top * factor, (TILE, HEAD_DIM))

    def finish(slot, i, head):
        here = pl.ds(head * HEAD_DIM, HEAD_DIM)
        named = listed(i, head)
        value_from = [jnp.where(n >= 0, n, window_tiles) for n in named]
        ones_from = [jnp.where(n >= 0, 1, 0) for n in named]
        top = jnp.concatenate([highest[slot]] * 2, axis=1)
        weights = [
            jnp.exp2(scores[slot, j] * factor - top).astype(jnp.bfloat16)
            for j in range(slots // 2)
        ]
        summed = jnp.dot(
            jnp.concatenate(weights, axis=1),
            jnp.concatenate(
                [
                    jnp.concatenate([value[v, :, here], counted[o]], axis=1)
                    for v, o in zip(value_from, ones_from)
                ],
                axis=0,
            ),
            preferred_element_type=jnp.float32,
        )
        result[i, :, here] = (summed[:, :HEAD_DIM] / summed[:, HEAD_DIM:]).astype(jnp.bfloat16)

    heads = width // HEAD_DIM
    together = tiles
    steps = [(tile, head) for tile in range(together) for head in range(heads)]
    score(0, 0, 0)

    def some_tiles(n, carry):
        first = n * together
        for number, (tile, head) in enumerate(steps):
            ahead_tile, ahead_head = (steps + [(together, 0)])[number + 1]
            score((number + 1) % 2, jnp.minimum(first + ahead_tile, tiles - 1), ahead_head)
            finish(number % 2, first + tile, head)
        return carry

    lax.fori_loop(0, tiles // together, some_tiles, 0)
    copy = pltpu.make_async_copy(
        result, out.at[pl.ds(first_tile, tiles)], sems.at[len(copies)]
    )
    copy.start()
    copy.wait()


def attend(lists, first_tile, own, halo, filled=()):
    heads, tiles, slots = lists.shape
    slab_tiles = own.shape[0]
    window_tiles = slab_tiles + REACH
    width = heads * HEAD_DIM
    pairs = heads * tiles * slots
    return pl.pallas_call(
        functools.partial(attend_kernel, first_tile, tiles, slots, len(filled)),
        in_specs=[pl.BlockSpec(memory_space=pltpu.SMEM)]
        + [pl.BlockSpec(memory_space=pl.ANY)] * (2 + len(filled)),
        out_specs=pl.BlockSpec(memory_space=pl.ANY),
        out_shape=jax.ShapeDtypeStruct((slab_tiles, TILE, width), jnp.bfloat16),
        scratch_shapes=[
            pltpu.VMEM((tiles, TILE, width), jnp.bfloat16),
            pltpu.VMEM((window_tiles, TILE, width), jnp.bfloat16),
            pltpu.VMEM((window_tiles + 1, TILE, width), jnp.bfloat16),
            pltpu.VMEM((2, TILE, HEAD_DIM), jnp.bfloat16),
            pltpu.VMEM((tiles, TILE, width), jnp.bfloat16),
            pltpu.VMEM((2, slots // 2, TILE, 2 * TILE), jnp.float32),
            pltpu.VMEM((2, TILE, HEAD_DIM), jnp.float32),
            pltpu.SemaphoreType.DMA((6,)),
        ],
        input_output_aliases={3: 0} if filled else {},
        compiler_params=pltpu.CompilerParams(vmem_limit_bytes=ATTEND_VMEM),
        cost_estimate=pl.CostEstimate(
            flops=4 * pairs * TILE * TILE * HEAD_DIM,
            bytes_accessed=2 * TILE * width * (2 * tiles + 2 * window_tiles),
            transcendentals=pairs * TILE * TILE,
        ),
        name="attend",
    )(lists.reshape(-1), own, halo, *filled)


def on_device(queries, keys, values, key_tiles, tile_mask):
    slab_tiles = key_tiles.shape[1]
    half = slab_tiles // 2
    groups = lax.axis_size("uly")
    slab = lax.axis_index("blk")
    turn = flipped(slab, lax.axis_size("blk")).astype(jnp.int32).reshape(1)
    lower = jnp.arange(slab_tiles)[:, None] < half
    window_start = slab * slab_tiles - jnp.where(lower, REACH, 0)
    lists = jnp.clip(key_tiles - window_start, 0, slab_tiles + REACH - 1)
    lists = to_holder(jnp.where(tile_mask > 0, lists, -1))
    received = []
    skipped = 0
    for heads in HEAD_SETS:
        width = heads * HEAD_DIM
        vmem = PACK_VMEM if received else FIRST_PACK_VMEM
        packed = pack((queries, keys, values), turn, groups, skipped, width, vmem)
        skipped += width
        if received:
            packed, received[-1], lists = lax.optimization_barrier((packed, received[-1], lists))
        received.append(exchanged(packed))
    results = []
    head = 0
    for heads, own in zip(HEAD_SETS, received):
        here = lists[head : head + heads]
        earlier = to_neighbour(own[slab_tiles - REACH :, 1:], 1)
        further = to_neighbour(own[:REACH, 1:], -1)
        attended = attend(here[:, :half], 0, own, earlier)
        attended = attend(here[:, half:], half, own, further, (attended,))
        results.append(exchanged(attended))
        head += heads
    return unpack(results, turn, groups)


def solution(mesh):
    placed = (
        P(("blk", "uly"), None),
        P(("blk", "uly"), None),
        P(("blk", "uly"), None),
        P("uly", "blk", None),
        P("uly", "blk", None),
    )
    return jax.shard_map(
        on_device, mesh=mesh, in_specs=placed, out_specs=P(("blk", "uly"), None), check_vma=False
    )
```

```python
import functools
import math

import jax
import jax.numpy as jnp
from jax import lax
from jax.experimental import pallas as pl
from jax.experimental.pallas import tpu as pltpu
from jax.sharding import PartitionSpec as P

TILE = 128
HEAD_DIM = 128
HEAD_SETS = (2, 1)
REACH = 8
PACK_VMEM = 8 * 1024 * 1024
FIRST_PACK_VMEM = 63 * 1024 * 1024
ATTEND_VMEM = 10 * 1024 * 1024


def flipped(slab, slabs):
    return slab // (slabs // 2)


def to_neighbour(x, by):
    slabs, groups = lax.axis_size("blk"), lax.axis_size("uly")
    pairs = []
    for slab in range(slabs):
        other = slab + by
        if 0 <= other < slabs:
            turn = flipped(slab, slabs) ^ flipped(other, slabs)
            for device in range(groups):
                pairs.append((slab * groups + device, other * groups + (device ^ turn)))
    return lax.ppermute(x, ("blk", "uly"), pairs)


def to_holder(x):
    slabs, groups = lax.axis_size("blk"), lax.axis_size("uly")
    pairs = [
        (slab * groups + device, slab * groups + (device ^ flipped(slab, slabs)))
        for slab in range(slabs)
        for device in range(groups)
    ]
    return lax.ppermute(x, ("blk", "uly"), pairs)


def exchanged(x):
    return lax.all_to_all(x, "uly", split_axis=0, concat_axis=0, tiled=True)


def pack_kernel(per_group, skipped, turn_ref, *refs):
    inputs, (out, held, arrived, left) = refs[:3], refs[3:]
    groups, width = out.shape[0], out.shape[-1]
    taken = [
        pltpu.make_async_copy(ref, held.at[which], arrived.at[which])
        for which, ref in enumerate(inputs)
    ]
    for copy in taken:
        copy.start()
    sent = []
    for which, copy in enumerate(taken):
        copy.wait()
        for group in range(groups):
            copy = pltpu.make_async_copy(
                held.at[which, :, pl.ds(group * per_group + skipped, width)],
                out.at[group ^ turn_ref[0], which],
                left.at[which, group],
            )
            copy.start()
            sent.append(copy)
    for copy in sent:
        copy.wait()


def pack(inputs, turn, groups, skipped, width, vmem):
    rows, columns = inputs[0].shape
    return pl.pallas_call(
        functools.partial(pack_kernel, columns // groups, skipped),
        in_specs=[pl.BlockSpec(memory_space=pltpu.SMEM)]
        + [pl.BlockSpec(memory_space=pltpu.HBM)] * 3,
        out_specs=pl.BlockSpec(memory_space=pltpu.HBM),
        out_shape=jax.ShapeDtypeStruct((groups, 3, rows, width), jnp.bfloat16),
        scratch_shapes=[
            pltpu.VMEM((3, rows, columns), jnp.bfloat16),
            pltpu.SemaphoreType.DMA((3,)),
            pltpu.SemaphoreType.DMA((3, groups)),
        ],
        compiler_params=pltpu.CompilerParams(vmem_limit_bytes=vmem),
        cost_estimate=pl.CostEstimate(
            flops=0, bytes_accessed=2 * 3 * rows * (columns + groups * width), transcendentals=0
        ),
        name="pack",
    )(turn, *inputs)


def unpack_kernel(widths, chunks, turn_ref, *refs):
    inputs, (out, held, sems) = refs[: len(widths)], refs[len(widths) :]
    groups, per_group = inputs[0].shape[0], sum(widths)
    per_chunk = groups // chunks
    copies = []
    for chunk in range(chunks):
        for group in range(chunk * per_chunk, (chunk + 1) * per_chunk):
            column = group * per_group
            for ref, width in zip(inputs, widths):
                held[:, column : column + width] = ref[group ^ turn_ref[0]]
                column += width
        here = pl.ds(chunk * per_chunk * per_group, per_chunk * per_group)
        copies.append(pltpu.make_async_copy(held.at[:, here], out.at[:, here], sems.at[chunk]))
        copies[-1].start()
    for copy in copies:
        copy.wait()


def unpack(parts, turn, groups):
    widths = [part.shape[-1] for part in parts]
    chunks = 4
    shape = (TILE, groups * sum(widths))
    return pl.pallas_call(
        functools.partial(unpack_kernel, widths, chunks),
        in_specs=[pl.BlockSpec(memory_space=pltpu.SMEM)]
        + [pl.BlockSpec(memory_space=pltpu.VMEM)] * len(parts),
        out_specs=pl.BlockSpec(memory_space=pl.ANY),
        out_shape=jax.ShapeDtypeStruct(shape, jnp.bfloat16),
        scratch_shapes=[pltpu.VMEM(shape, jnp.bfloat16), pltpu.SemaphoreType.DMA((chunks,))],
        compiler_params=pltpu.CompilerParams(vmem_limit_bytes=PACK_VMEM),
        name="unpack",
    )(turn, *parts)


def attend_kernel(first_tile, tiles, slots, n_filled, list_ref, own, halo, *refs):
    out, query, key, value, counted, result, scores, highest, sems = refs[n_filled:]
    slab_tiles, _, _, width = own.shape
    window_tiles = slab_tiles + REACH
    halo_at, own_at = (0, REACH) if first_tile == 0 else (slab_tiles, 0)
    centre = first_tile + own_at
    copies = [pltpu.make_async_copy(own.at[pl.ds(first_tile, tiles), 0], query, sems.at[0])]
    for source, first, where in (
        (halo, 0, pl.ds(halo_at, REACH)),
        (own, 1, pl.ds(own_at, slab_tiles)),
    ):
        for which, window in enumerate((key, value)):
            copies.append(
                pltpu.make_async_copy(
                    source.at[:, first + which], window.at[where], sems.at[len(copies)]
                )
            )
    for copy in copies:
        copy.start()
    value[window_tiles] = jnp.zeros((TILE, width), jnp.bfloat16)
    counted[0] = jnp.zeros((TILE, HEAD_DIM), jnp.bfloat16)
    counted[1] = jnp.ones((TILE, HEAD_DIM), jnp.bfloat16)
    for copy in copies:
        copy.wait()
    factor = math.log2(math.e) / math.sqrt(HEAD_DIM)

    def listed(i, head):
        return [list_ref[(head * tiles + i) * slots + j] for j in range(slots)]

    def score(slot, i, head):
        here = pl.ds(head * HEAD_DIM, HEAD_DIM)
        key_from = [jnp.where(n >= 0, n, i + centre) for n in listed(i, head)]
        tile_queries = query[i, :, here]
        products = []
        for j in range(0, slots, 2):
            both = jnp.concatenate([key[key_from[j], :, here], key[key_from[j + 1], :, here]], axis=0)
            product = lax.dot_general(
                tile_queries, both, (((1,), (1,)), ((), ())), preferred_element_type=jnp.float32
            )
            scores[slot, j // 2] = product
            products.append(product)
        top = jnp.max(functools.reduce(jnp.maximum, products), axis=1, keepdims=True)
        highest[slot] = jnp.broadcast_to(top * factor, (TILE, HEAD_DIM))

    def finish(slot, i, head):
        here = pl.ds(head * HEAD_DIM, HEAD_DIM)
        named = listed(i, head)
        value_from = [jnp.where(n >= 0, n, window_tiles) for n in named]
        ones_from = [jnp.where(n >= 0, 1, 0) for n in named]
        top = jnp.concatenate([highest[slot]] * 2, axis=1)
        weights = [
            jnp.exp2(scores[slot, j] * factor - top).astype(jnp.bfloat16)
            for j in range(slots // 2)
        ]
        summed = jnp.dot(
            jnp.concatenate(weights, axis=1),
            jnp.concatenate(
                [
                    jnp.concatenate([value[v, :, here], counted[o]], axis=1)
                    for v, o in zip(value_from, ones_from)
                ],
                axis=0,
            ),
            preferred_element_type=jnp.float32,
        )
        result[i, :, here] = (summed[:, :HEAD_DIM] / summed[:, HEAD_DIM:]).astype(jnp.bfloat16)

    heads = width // HEAD_DIM
    together = tiles
    steps = [(tile, head) for tile in range(together) for head in range(heads)]
    score(0, 0, 0)

    def some_tiles(n, carry):
        first = n * together
        for number, (tile, head) in enumerate(steps):
            ahead_tile, ahead_head = (steps + [(together, 0)])[number + 1]
            score((number + 1) % 2, jnp.minimum(first + ahead_tile, tiles - 1), ahead_head)
            finish(number % 2, first + tile, head)
        return carry

    lax.fori_loop(0, tiles // together, some_tiles, 0)
    copy = pltpu.make_async_copy(
        result, out.at[pl.ds(first_tile, tiles)], sems.at[len(copies)]
    )
    copy.start()
    copy.wait()


def attend(lists, first_tile, own, halo, filled=()):
    heads, tiles, slots = lists.shape
    slab_tiles = own.shape[0]
    window_tiles = slab_tiles + REACH
    width = heads * HEAD_DIM
    pairs = heads * tiles * slots
    return pl.pallas_call(
        functools.partial(attend_kernel, first_tile, tiles, slots, len(filled)),
        in_specs=[pl.BlockSpec(memory_space=pltpu.SMEM)]
        + [pl.BlockSpec(memory_space=pl.ANY)] * (2 + len(filled)),
        out_specs=pl.BlockSpec(memory_space=pl.ANY),
        out_shape=jax.ShapeDtypeStruct((slab_tiles, TILE, width), jnp.bfloat16),
        scratch_shapes=[
            pltpu.VMEM((tiles, TILE, width), jnp.bfloat16),
            pltpu.VMEM((window_tiles, TILE, width), jnp.bfloat16),
            pltpu.VMEM((window_tiles + 1, TILE, width), jnp.bfloat16),
            pltpu.VMEM((2, TILE, HEAD_DIM), jnp.bfloat16),
            pltpu.VMEM((tiles, TILE, width), jnp.bfloat16),
            pltpu.VMEM((2, slots // 2, TILE, 2 * TILE), jnp.float32),
            pltpu.VMEM((2, TILE, HEAD_DIM), jnp.float32),
            pltpu.SemaphoreType.DMA((6,)),
        ],
        input_output_aliases={3: 0} if filled else {},
        compiler_params=pltpu.CompilerParams(vmem_limit_bytes=ATTEND_VMEM),
        cost_estimate=pl.CostEstimate(
            flops=4 * pairs * TILE * TILE * HEAD_DIM,
            bytes_accessed=2 * TILE * width * (2 * tiles + 2 * window_tiles),
            transcendentals=pairs * TILE * TILE,
        ),
        name="attend",
    )(lists.reshape(-1), own, halo, *filled)


def on_device(queries, keys, values, key_tiles, tile_mask):
    slab_tiles = key_tiles.shape[1]
    half = slab_tiles // 2
    groups = lax.axis_size("uly")
    slab = lax.axis_index("blk")
    turn = flipped(slab, lax.axis_size("blk")).astype(jnp.int32).reshape(1)
    lower = jnp.arange(slab_tiles)[:, None] < half
    window_start = slab * slab_tiles - jnp.where(lower, REACH, 0)
    lists = jnp.clip(key_tiles - window_start, 0, slab_tiles + REACH - 1)
    lists = to_holder(jnp.where(tile_mask > 0, lists, -1))
    received = []
    skipped = 0
    for heads in HEAD_SETS:
        width = heads * HEAD_DIM
        vmem = PACK_VMEM if received else FIRST_PACK_VMEM
        packed = pack((queries, keys, values), turn, groups, skipped, width, vmem)
        skipped += width
        if received:
            packed, received[-1], lists = lax.optimization_barrier((packed, received[-1], lists))
        received.append(exchanged(packed))
    results = []
    head = 0
    for heads, own in zip(HEAD_SETS, received):
        here = lists[head : head + heads]
        earlier = to_neighbour(own[slab_tiles - REACH :, 1:], 1)
        further = to_neighbour(own[:REACH, 1:], -1)
        attended = attend(here[:, :half], 0, own, earlier)
        attended = attend(here[:, half:], half, own, further, (attended,))
        results.append(exchanged(attended))
        head += heads
    return unpack(results, turn, groups)


def solution(mesh):
    placed = (
        P(("blk", "uly"), None),
        P(("blk", "uly"), None),
        P(("blk", "uly"), None),
        P("uly", "blk", None),
        P("uly", "blk", None),
    )
    return jax.shard_map(
        on_device, mesh=mesh, in_specs=placed, out_specs=P(("blk", "uly"), None), check_vma=False
    )
```

```python
import functools
import math

import jax
import jax.numpy as jnp
from jax import lax
from jax.experimental import pallas as pl
from jax.experimental.pallas import tpu as pltpu
from jax.sharding import PartitionSpec as P

TILE = 128
HEAD_DIM = 128
HEAD_SETS = (2, 1)
REACH = 8
PACK_VMEM = 8 * 1024 * 1024
FIRST_PACK_VMEM = 63 * 1024 * 1024
ATTEND_VMEM = 20 * 1024 * 1024


def flipped(slab, slabs):
    return slab // (slabs // 2)


def to_neighbour(x, by):
    slabs, groups = lax.axis_size("blk"), lax.axis_size("uly")
    pairs = []
    for slab in range(slabs):
        other = slab + by
        if 0 <= other < slabs:
            turn = flipped(slab, slabs) ^ flipped(other, slabs)
            for device in range(groups):
                pairs.append((slab * groups + device, other * groups + (device ^ turn)))
    return lax.ppermute(x, ("blk", "uly"), pairs)


def to_holder(x):
    slabs, groups = lax.axis_size("blk"), lax.axis_size("uly")
    pairs = [
        (slab * groups + device, slab * groups + (device ^ flipped(slab, slabs)))
        for slab in range(slabs)
        for device in range(groups)
    ]
    return lax.ppermute(x, ("blk", "uly"), pairs)


def exchanged(x):
    return lax.all_to_all(x, "uly", split_axis=0, concat_axis=0, tiled=True)


def pack_kernel(per_group, skipped, turn_ref, *refs):
    inputs, (out, held, arrived, left) = refs[:3], refs[3:]
    groups, width = out.shape[0], out.shape[-1]
    taken = [
        pltpu.make_async_copy(ref, held.at[which], arrived.at[which])
        for which, ref in enumerate(inputs)
    ]
    for copy in taken:
        copy.start()
    sent = []
    for which, copy in enumerate(taken):
        copy.wait()
        for group in range(groups):
            copy = pltpu.make_async_copy(
                held.at[which, :, pl.ds(group * per_group + skipped, width)],
                out.at[group ^ turn_ref[0], which],
                left.at[which, group],
            )
            copy.start()
            sent.append(copy)
    for copy in sent:
        copy.wait()


def pack(inputs, turn, groups, skipped, width, vmem):
    rows, columns = inputs[0].shape
    return pl.pallas_call(
        functools.partial(pack_kernel, columns // groups, skipped),
        in_specs=[pl.BlockSpec(memory_space=pltpu.SMEM)]
        + [pl.BlockSpec(memory_space=pltpu.HBM)] * 3,
        out_specs=pl.BlockSpec(memory_space=pltpu.HBM),
        out_shape=jax.ShapeDtypeStruct((groups, 3, rows, width), jnp.bfloat16),
        scratch_shapes=[
            pltpu.VMEM((3, rows, columns), jnp.bfloat16),
            pltpu.SemaphoreType.DMA((3,)),
            pltpu.SemaphoreType.DMA((3, groups)),
        ],
        compiler_params=pltpu.CompilerParams(vmem_limit_bytes=vmem),
        cost_estimate=pl.CostEstimate(
            flops=0, bytes_accessed=2 * 3 * rows * (columns + groups * width), transcendentals=0
        ),
        name="pack",
    )(turn, *inputs)


def unpack_kernel(widths, chunks, turn_ref, *refs):
    inputs, (out, held, sems) = refs[: len(widths)], refs[len(widths) :]
    groups, per_group = inputs[0].shape[0], sum(widths)
    per_chunk = groups // chunks
    copies = []
    for chunk in range(chunks):
        for group in range(chunk * per_chunk, (chunk + 1) * per_chunk):
            column = group * per_group
            for ref, width in zip(inputs, widths):
                held[:, column : column + width] = ref[group ^ turn_ref[0]]
                column += width
        here = pl.ds(chunk * per_chunk * per_group, per_chunk * per_group)
        copies.append(pltpu.make_async_copy(held.at[:, here], out.at[:, here], sems.at[chunk]))
        copies[-1].start()
    for copy in copies:
        copy.wait()


def unpack(parts, turn, groups):
    widths = [part.shape[-1] for part in parts]
    chunks = 4
    shape = (TILE, groups * sum(widths))
    return pl.pallas_call(
        functools.partial(unpack_kernel, widths, chunks),
        in_specs=[pl.BlockSpec(memory_space=pltpu.SMEM)]
        + [pl.BlockSpec(memory_space=pltpu.VMEM)] * len(parts),
        out_specs=pl.BlockSpec(memory_space=pl.ANY),
        out_shape=jax.ShapeDtypeStruct(shape, jnp.bfloat16),
        scratch_shapes=[pltpu.VMEM(shape, jnp.bfloat16), pltpu.SemaphoreType.DMA((chunks,))],
        compiler_params=pltpu.CompilerParams(vmem_limit_bytes=PACK_VMEM),
        name="unpack",
    )(turn, *parts)


def attend_kernel(first_tile, tiles, slots, n_filled, list_ref, own, halo, *refs):
    out, query, key, value, counted, result, scores, highest, sems = refs[n_filled:]
    slab_tiles, _, _, width = own.shape
    window_tiles = slab_tiles + REACH
    halo_at, own_at = (0, REACH) if first_tile == 0 else (slab_tiles, 0)
    centre = first_tile + own_at
    copies = [pltpu.make_async_copy(own.at[pl.ds(first_tile, tiles), 0], query, sems.at[0])]
    for source, first, where in (
        (halo, 0, pl.ds(halo_at, REACH)),
        (own, 1, pl.ds(own_at, slab_tiles)),
    ):
        for which, window in enumerate((key, value)):
            copies.append(
                pltpu.make_async_copy(
                    source.at[:, first + which], window.at[where], sems.at[len(copies)]
                )
            )
    for copy in copies:
        copy.start()
    value[window_tiles] = jnp.zeros((TILE, width), jnp.bfloat16)
    counted[0] = jnp.zeros((TILE, HEAD_DIM), jnp.bfloat16)
    counted[1] = jnp.ones((TILE, HEAD_DIM), jnp.bfloat16)
    for copy in copies:
        copy.wait()
    factor = math.log2(math.e) / math.sqrt(HEAD_DIM)

    def listed(i, head):
        return [list_ref[(head * tiles + i) * slots + j] for j in range(slots)]

    def score(slot, i, head):
        here = pl.ds(head * HEAD_DIM, HEAD_DIM)
        key_from = [jnp.where(n >= 0, n, i + centre) for n in listed(i, head)]
        tile_queries = query[i, :, here]
        products = []
        for j in range(0, slots, 2):
            both = jnp.concatenate([key[key_from[j], :, here], key[key_from[j + 1], :, here]], axis=0)
            product = lax.dot_general(
                tile_queries, both, (((1,), (1,)), ((), ())), preferred_element_type=jnp.float32
            )
            scores[slot, j // 2] = product
            products.append(product)
        top = jnp.max(functools.reduce(jnp.maximum, products), axis=1, keepdims=True)
        highest[slot] = jnp.broadcast_to(top * factor, (TILE, HEAD_DIM))

    def finish(slot, i, head):
        here = pl.ds(head * HEAD_DIM, HEAD_DIM)
        named = listed(i, head)
        value_from = [jnp.where(n >= 0, n, window_tiles) for n in named]
        ones_from = [jnp.where(n >= 0, 1, 0) for n in named]
        top = jnp.concatenate([highest[slot]] * 2, axis=1)
        weights = [
            jnp.exp2(scores[slot, j] * factor - top).astype(jnp.bfloat16)
            for j in range(slots // 2)
        ]
        summed = jnp.dot(
            jnp.concatenate(weights, axis=1),
            jnp.concatenate(
                [
                    jnp.concatenate([value[v, :, here], counted[o]], axis=1)
                    for v, o in zip(value_from, ones_from)
                ],
                axis=0,
            ),
            preferred_element_type=jnp.float32,
        )
        result[i, :, here] = (summed[:, :HEAD_DIM] / summed[:, HEAD_DIM:]).astype(jnp.bfloat16)

    heads = width // HEAD_DIM
    together = tiles
    steps = [(tile, head) for tile in range(together) for head in range(heads)]
    score(0, 0, 0)

    def some_tiles(n, carry):
        first = n * together
        for number, (tile, head) in enumerate(steps):
            ahead_tile, ahead_head = (steps + [(together, 0)])[number + 1]
            score((number + 1) % 2, jnp.minimum(first + ahead_tile, tiles - 1), ahead_head)
            finish(number % 2, first + tile, head)
        return carry

    lax.fori_loop(0, tiles // together, some_tiles, 0)
    copy = pltpu.make_async_copy(
        result, out.at[pl.ds(first_tile, tiles)], sems.at[len(copies)]
    )
    copy.start()
    copy.wait()


def attend(lists, first_tile, own, halo, filled=()):
    heads, tiles, slots = lists.shape
    slab_tiles = own.shape[0]
    window_tiles = slab_tiles + REACH
    width = heads * HEAD_DIM
    pairs = heads * tiles * slots
    return pl.pallas_call(
        functools.partial(attend_kernel, first_tile, tiles, slots, len(filled)),
        in_specs=[pl.BlockSpec(memory_space=pltpu.SMEM)]
        + [pl.BlockSpec(memory_space=pltpu.VMEM)] * 2
        + [pl.BlockSpec(memory_space=pl.ANY)] * len(filled),
        out_specs=pl.BlockSpec(memory_space=pl.ANY),
        out_shape=jax.ShapeDtypeStruct((slab_tiles, TILE, width), jnp.bfloat16),
        scratch_shapes=[
            pltpu.VMEM((tiles, TILE, width), jnp.bfloat16),
            pltpu.VMEM((window_tiles, TILE, width), jnp.bfloat16),
            pltpu.VMEM((window_tiles + 1, TILE, width), jnp.bfloat16),
            pltpu.VMEM((2, TILE, HEAD_DIM), jnp.bfloat16),
            pltpu.VMEM((tiles, TILE, width), jnp.bfloat16),
            pltpu.VMEM((2, slots // 2, TILE, 2 * TILE), jnp.float32),
            pltpu.VMEM((2, TILE, HEAD_DIM), jnp.float32),
            pltpu.SemaphoreType.DMA((6,)),
        ],
        input_output_aliases={3: 0} if filled else {},
        compiler_params=pltpu.CompilerParams(vmem_limit_bytes=ATTEND_VMEM),
        cost_estimate=pl.CostEstimate(
            flops=4 * pairs * TILE * TILE * HEAD_DIM,
            bytes_accessed=2 * TILE * width * (2 * tiles + 2 * window_tiles),
            transcendentals=pairs * TILE * TILE,
        ),
        name="attend",
    )(lists.reshape(-1), own, halo, *filled)


def on_device(queries, keys, values, key_tiles, tile_mask):
    slab_tiles = key_tiles.shape[1]
    half = slab_tiles // 2
    groups = lax.axis_size("uly")
    slab = lax.axis_index("blk")
    turn = flipped(slab, lax.axis_size("blk")).astype(jnp.int32).reshape(1)
    lower = jnp.arange(slab_tiles)[:, None] < half
    window_start = slab * slab_tiles - jnp.where(lower, REACH, 0)
    lists = jnp.clip(key_tiles - window_start, 0, slab_tiles + REACH - 1)
    lists = to_holder(jnp.where(tile_mask > 0, lists, -1))
    received = []
    skipped = 0
    for heads in HEAD_SETS:
        width = heads * HEAD_DIM
        vmem = PACK_VMEM if received else FIRST_PACK_VMEM
        packed = pack((queries, keys, values), turn, groups, skipped, width, vmem)
        skipped += width
        if received:
            packed, received[-1], lists = lax.optimization_barrier((packed, received[-1], lists))
        received.append(exchanged(packed))
    results = []
    head = 0
    for heads, own in zip(HEAD_SETS, received):
        here = lists[head : head + heads]
        earlier = to_neighbour(own[slab_tiles - REACH :, 1:], 1)
        further = to_neighbour(own[:REACH, 1:], -1)
        attended = attend(here[:, :half], 0, own, earlier)
        attended = attend(here[:, half:], half, own, further, (attended,))
        results.append(exchanged(attended))
        head += heads
    return unpack(results, turn, groups)


def solution(mesh):
    placed = (
        P(("blk", "uly"), None),
        P(("blk", "uly"), None),
        P(("blk", "uly"), None),
        P("uly", "blk", None),
        P("uly", "blk", None),
    )
    return jax.shard_map(
        on_device, mesh=mesh, in_specs=placed, out_specs=P(("blk", "uly"), None), check_vma=False
    )
```

```python
import functools
import math

import jax
import jax.numpy as jnp
from jax import lax
from jax.experimental import pallas as pl
from jax.experimental.pallas import tpu as pltpu
from jax.sharding import PartitionSpec as P

TILE = 128
HEAD_DIM = 128
HEAD_SETS = (2, 1)
REACH = 8
PACK_VMEM = 8 * 1024 * 1024
FIRST_PACK_VMEM = 63 * 1024 * 1024
ATTEND_VMEM = 20 * 1024 * 1024


def flipped(slab, slabs):
    return slab // (slabs // 2)


def to_neighbour(x, by):
    slabs, groups = lax.axis_size("blk"), lax.axis_size("uly")
    pairs = []
    for slab in range(slabs):
        other = slab + by
        if 0 <= other < slabs:
            turn = flipped(slab, slabs) ^ flipped(other, slabs)
            for device in range(groups):
                pairs.append((slab * groups + device, other * groups + (device ^ turn)))
    return lax.ppermute(x, ("blk", "uly"), pairs)


def to_holder(x):
    slabs, groups = lax.axis_size("blk"), lax.axis_size("uly")
    pairs = [
        (slab * groups + device, slab * groups + (device ^ flipped(slab, slabs)))
        for slab in range(slabs)
        for device in range(groups)
    ]
    return lax.ppermute(x, ("blk", "uly"), pairs)


def exchanged(x):
    return lax.all_to_all(x, "uly", split_axis=0, concat_axis=0, tiled=True)


def pack_kernel(per_group, skipped, turn_ref, *refs):
    inputs, (out, held, arrived, left) = refs[:3], refs[3:]
    groups, width = out.shape[0], out.shape[-1]
    taken = [
        pltpu.make_async_copy(ref, held.at[which], arrived.at[which])
        for which, ref in enumerate(inputs)
    ]
    for copy in taken:
        copy.start()
    sent = []
    for which, copy in enumerate(taken):
        copy.wait()
        for group in range(groups):
            copy = pltpu.make_async_copy(
                held.at[which, :, pl.ds(group * per_group + skipped, width)],
                out.at[group ^ turn_ref[0], which],
                left.at[which, group],
            )
            copy.start()
            sent.append(copy)
    for copy in sent:
        copy.wait()


def pack(inputs, turn, groups, skipped, width, vmem):
    rows, columns = inputs[0].shape
    return pl.pallas_call(
        functools.partial(pack_kernel, columns // groups, skipped),
        in_specs=[pl.BlockSpec(memory_space=pltpu.SMEM)]
        + [pl.BlockSpec(memory_space=pltpu.HBM)] * 3,
        out_specs=pl.BlockSpec(memory_space=pltpu.HBM),
        out_shape=jax.ShapeDtypeStruct((groups, 3, rows, width), jnp.bfloat16),
        scratch_shapes=[
            pltpu.VMEM((3, rows, columns), jnp.bfloat16),
            pltpu.SemaphoreType.DMA((3,)),
            pltpu.SemaphoreType.DMA((3, groups)),
        ],
        compiler_params=pltpu.CompilerParams(vmem_limit_bytes=vmem),
        cost_estimate=pl.CostEstimate(
            flops=0, bytes_accessed=2 * 3 * rows * (columns + groups * width), transcendentals=0
        ),
        name="pack",
    )(turn, *inputs)


def unpack_kernel(widths, chunks, turn_ref, *refs):
    inputs, (out, held, sems) = refs[: len(widths)], refs[len(widths) :]
    groups, per_group = inputs[0].shape[0], sum(widths)
    per_chunk = groups // chunks
    copies = []
    for chunk in range(chunks):
        for group in range(chunk * per_chunk, (chunk + 1) * per_chunk):
            column = group * per_group
            for ref, width in zip(inputs, widths):
                held[:, column : column + width] = ref[group ^ turn_ref[0]]
                column += width
        here = pl.ds(chunk * per_chunk * per_group, per_chunk * per_group)
        copies.append(pltpu.make_async_copy(held.at[:, here], out.at[:, here], sems.at[chunk]))
        copies[-1].start()
    for copy in copies:
        copy.wait()


def unpack(parts, turn, groups):
    widths = [part.shape[-1] for part in parts]
    chunks = 4
    shape = (TILE, groups * sum(widths))
    return pl.pallas_call(
        functools.partial(unpack_kernel, widths, chunks),
        in_specs=[pl.BlockSpec(memory_space=pltpu.SMEM)]
        + [pl.BlockSpec(memory_space=pltpu.VMEM)] * len(parts),
        out_specs=pl.BlockSpec(memory_space=pl.ANY),
        out_shape=jax.ShapeDtypeStruct(shape, jnp.bfloat16),
        scratch_shapes=[pltpu.VMEM(shape, jnp.bfloat16), pltpu.SemaphoreType.DMA((chunks,))],
        compiler_params=pltpu.CompilerParams(vmem_limit_bytes=PACK_VMEM),
        name="unpack",
    )(turn, *parts)


def attend_kernel(first_tile, tiles, slots, n_filled, list_ref, own, halo, *refs):
    out, query, key, value, counted, result, scores, highest, sems = refs[n_filled:]
    slab_tiles, _, _, width = own.shape
    window_tiles = slab_tiles + REACH
    halo_at, own_at = (0, REACH) if first_tile == 0 else (slab_tiles, 0)
    centre = first_tile + own_at
    copies = [pltpu.make_async_copy(own.at[pl.ds(first_tile, tiles), 0], query, sems.at[0])]
    for source, first, where in (
        (halo, 0, pl.ds(halo_at, REACH)),
        (own, 1, pl.ds(own_at, slab_tiles)),
    ):
        for which, window in enumerate((key, value)):
            copies.append(
                pltpu.make_async_copy(
                    source.at[:, first + which], window.at[where], sems.at[len(copies)]
                )
            )
    for copy in copies:
        copy.start()
    value[window_tiles] = jnp.zeros((TILE, width), jnp.bfloat16)
    counted[0] = jnp.zeros((TILE, HEAD_DIM), jnp.bfloat16)
    counted[1] = jnp.ones((TILE, HEAD_DIM), jnp.bfloat16)
    for copy in (copies[0], copies[1], copies[3]):
        copy.wait()
    factor = math.log2(math.e) / math.sqrt(HEAD_DIM)

    def listed(i, head):
        return [list_ref[(head * tiles + i) * slots + j] for j in range(slots)]

    def score(slot, i, head):
        here = pl.ds(head * HEAD_DIM, HEAD_DIM)
        key_from = [jnp.where(n >= 0, n, i + centre) for n in listed(i, head)]
        tile_queries = query[i, :, here]
        products = []
        for j in range(0, slots, 2):
            both = jnp.concatenate([key[key_from[j], :, here], key[key_from[j + 1], :, here]], axis=0)
            product = lax.dot_general(
                tile_queries, both, (((1,), (1,)), ((), ())), preferred_element_type=jnp.float32
            )
            scores[slot, j // 2] = product
            products.append(product)
        top = jnp.max(functools.reduce(jnp.maximum, products), axis=1, keepdims=True)
        highest[slot] = jnp.broadcast_to(top * factor, (TILE, HEAD_DIM))

    def finish(slot, i, head):
        here = pl.ds(head * HEAD_DIM, HEAD_DIM)
        named = listed(i, head)
        value_from = [jnp.where(n >= 0, n, window_tiles) for n in named]
        ones_from = [jnp.where(n >= 0, 1, 0) for n in named]
        top = jnp.concatenate([highest[slot]] * 2, axis=1)
        weights = [
            jnp.exp2(scores[slot, j] * factor - top).astype(jnp.bfloat16)
            for j in range(slots // 2)
        ]
        summed = jnp.dot(
            jnp.concatenate(weights, axis=1),
            jnp.concatenate(
                [
                    jnp.concatenate([value[v, :, here], counted[o]], axis=1)
                    for v, o in zip(value_from, ones_from)
                ],
                axis=0,
            ),
            preferred_element_type=jnp.float32,
        )
        result[i, :, here] = (summed[:, :HEAD_DIM] / summed[:, HEAD_DIM:]).astype(jnp.bfloat16)

    heads = width // HEAD_DIM
    together = tiles
    steps = [(tile, head) for tile in range(together) for head in range(heads)]
    score(0, 0, 0)
    for copy in (copies[2], copies[4]):
        copy.wait()

    def some_tiles(n, carry):
        first = n * together
        for number, (tile, head) in enumerate(steps):
            ahead_tile, ahead_head = (steps + [(together, 0)])[number + 1]
            score((number + 1) % 2, jnp.minimum(first + ahead_tile, tiles - 1), ahead_head)
            finish(number % 2, first + tile, head)
        return carry

    lax.fori_loop(0, tiles // together, some_tiles, 0)
    copy = pltpu.make_async_copy(
        result, out.at[pl.ds(first_tile, tiles)], sems.at[len(copies)]
    )
    copy.start()
    copy.wait()


def attend(lists, first_tile, own, halo, filled=()):
    heads, tiles, slots = lists.shape
    slab_tiles = own.shape[0]
    window_tiles = slab_tiles + REACH
    width = heads * HEAD_DIM
    pairs = heads * tiles * slots
    return pl.pallas_call(
        functools.partial(attend_kernel, first_tile, tiles, slots, len(filled)),
        in_specs=[pl.BlockSpec(memory_space=pltpu.SMEM)]
        + [pl.BlockSpec(memory_space=pltpu.VMEM)] * 2
        + [pl.BlockSpec(memory_space=pl.ANY)] * len(filled),
        out_specs=pl.BlockSpec(memory_space=pl.ANY),
        out_shape=jax.ShapeDtypeStruct((slab_tiles, TILE, width), jnp.bfloat16),
        scratch_shapes=[
            pltpu.VMEM((tiles, TILE, width), jnp.bfloat16),
            pltpu.VMEM((window_tiles, TILE, width), jnp.bfloat16),
            pltpu.VMEM((window_tiles + 1, TILE, width), jnp.bfloat16),
            pltpu.VMEM((2, TILE, HEAD_DIM), jnp.bfloat16),
            pltpu.VMEM((tiles, TILE, width), jnp.bfloat16),
            pltpu.VMEM((2, slots // 2, TILE, 2 * TILE), jnp.float32),
            pltpu.VMEM((2, TILE, HEAD_DIM), jnp.float32),
            pltpu.SemaphoreType.DMA((6,)),
        ],
        input_output_aliases={3: 0} if filled else {},
        compiler_params=pltpu.CompilerParams(vmem_limit_bytes=ATTEND_VMEM),
        cost_estimate=pl.CostEstimate(
            flops=4 * pairs * TILE * TILE * HEAD_DIM,
            bytes_accessed=2 * TILE * width * (2 * tiles + 2 * window_tiles),
            transcendentals=pairs * TILE * TILE,
        ),
        name="attend",
    )(lists.reshape(-1), own, halo, *filled)


def on_device(queries, keys, values, key_tiles, tile_mask):
    slab_tiles = key_tiles.shape[1]
    half = slab_tiles // 2
    groups = lax.axis_size("uly")
    slab = lax.axis_index("blk")
    turn = flipped(slab, lax.axis_size("blk")).astype(jnp.int32).reshape(1)
    lower = jnp.arange(slab_tiles)[:, None] < half
    window_start = slab * slab_tiles - jnp.where(lower, REACH, 0)
    lists = jnp.clip(key_tiles - window_start, 0, slab_tiles + REACH - 1)
    lists = to_holder(jnp.where(tile_mask > 0, lists, -1))
    received = []
    skipped = 0
    for heads in HEAD_SETS:
        width = heads * HEAD_DIM
        vmem = PACK_VMEM if received else FIRST_PACK_VMEM
        packed = pack((queries, keys, values), turn, groups, skipped, width, vmem)
        skipped += width
        if received:
            packed, received[-1], lists = lax.optimization_barrier((packed, received[-1], lists))
        received.append(exchanged(packed))
    results = []
    head = 0
    for heads, own in zip(HEAD_SETS, received):
        here = lists[head : head + heads]
        earlier = to_neighbour(own[slab_tiles - REACH :, 1:], 1)
        further = to_neighbour(own[:REACH, 1:], -1)
        attended = attend(here[:, :half], 0, own, earlier)
        attended = attend(here[:, half:], half, own, further, (attended,))
        results.append(exchanged(attended))
        head += heads
    return unpack(results, turn, groups)


def solution(mesh):
    placed = (
        P(("blk", "uly"), None),
        P(("blk", "uly"), None),
        P(("blk", "uly"), None),
        P("uly", "blk", None),
        P("uly", "blk", None),
    )
    return jax.shard_map(
        on_device, mesh=mesh, in_specs=placed, out_specs=P(("blk", "uly"), None), check_vma=False
    )
```
